32 devices in a mesh: tm: 4 (over z), height: 8 (over y, x, core).
Axes of the slice: x: 2, y: 2, z: 4, core: 2. Of those that a mesh axis runs over, the one named last changes fastest.
Arguments:
- latents: bfloat16 [9, 16, 128, 384], P(None, 'height', 'tm'), may hold values from -6 to 6
- gain_in: float32 [384], replicated, may hold values from 0.1 to 1.9
- weight_in: bfloat16 [3, 3, 3, 384, 384], replicated, may hold values from -0.0625 to 0.0625
- bias_in: float32 [384], replicated, may hold values from -3 to 3
- gain_mid: float32 [384], replicated, may hold values from 0.1 to 1.9
- weight_mid: bfloat16 [3, 3, 3, 384, 384], replicated, may hold values from -0.0625 to 0.0625
- bias_mid: float32 [384], replicated, may hold values from -2 to 2
- up_weight: bfloat16 [3, 3, 384, 192], replicated, may hold values from -0.109375 to 0.109375
- up_bias: float32 [192], replicated, may hold values from -2 to 2
Outputs:
- first_image: bfloat16 [32, 256, 192], P('height', 'tm')
- later_images: bfloat16 [8, 32, 256, 192], P('tm', 'height')
The draws below stay inside these ranges and needn't reach their ends.
All inputs are finite; a program needn't handle non-finite values.
Results may differ from the reference program's by a relative error of at most 0.0053.
Values may be sent and summed in bfloat16 or wider, within the bound.
A program may use at most 128 MiB of HBM per device.

```python
import jax
import jax.numpy as jnp
from jax import lax

CH = 384
CH_UP = 192
W = 128
H = 16
FRAMES = 9


def level_of(own_key, dims, cuts, least, top_value):
    factor_of, own = 1.0, jax.random.fold_in(own_key, 6)
    for dim, shards_of in cuts:
        heights = jnp.exp(jax.random.uniform(jax.random.fold_in(own, dim), (shards_of,), jnp.float32, least / len(cuts), top_value / len(cuts)))
        factor_of = factor_of * jnp.repeat(heights, dims[dim] // shards_of).reshape([-1 if axis == dim else 1 for axis in range(len(dims))])
    return factor_of


def noise(own_key, dims, deviation, most, split=(), dtype=jnp.bfloat16):
    values = jax.random.normal(own_key, dims, jnp.float32) * deviation
    if len(split) > 0:
        values = level_of(own_key, dims, split, -0.22, 0.18) * values
    return jnp.clip(values, min=-most, max=most).astype(dtype)


def setup_inputs(seed: int = 0) -> dict:
    streams_of = jax.random.split(jax.random.key(seed), 10)
    return {
        "latents": noise(streams_of[0], (FRAMES, H, W, CH), 1.0, 6.0, ((1, 8), (2, 4))),
        "gain_in": jnp.clip(1.0 + 0.18 * jax.random.normal(streams_of[1], (CH,), jnp.float32), 0.1, 1.9),
        "weight_in": noise(streams_of[2], (3, 3, 3, CH, CH), (27 * CH) ** -0.5, 0.0625),
        "bias_in": noise(streams_of[3], (CH,), 0.5, 3.0, (), jnp.float32),
        "gain_mid": jnp.clip(1.0 + 0.18 * jax.random.normal(streams_of[4], (CH,), jnp.float32), 0.1, 1.9),
        "weight_mid": noise(streams_of[5], (3, 3, 3, CH, CH), (27 * CH) ** -0.5, 0.0625),
        "bias_mid": noise(streams_of[6], (CH,), 0.3, 2.0, (), jnp.float32),
        "up_weight": noise(streams_of[7], (3, 3, CH, CH_UP), (9 * CH) ** -0.5, 0.109375),
        "up_bias": noise(streams_of[8], (CH_UP,), 0.3, 2.0, (), jnp.float32),
    }


epsilon = 1e-06

def normed_silu(values, norm_gain):
    factor = lax.rsqrt(lax.optimization_barrier(jnp.mean(values * values, axis=-1, keepdims=True)) + epsilon)
    return jax.nn.silu(values * factor * norm_gain)

def causal_volume(inputs, weight):
    padded = jnp.pad(inputs.astype(jnp.float32), ((2, 0), (1, 1), (1, 1), (0, 0)))
    output = lax.conv_general_dilated(padded[None], weight.astype(jnp.float32), (1, 1, 1), 'VALID', dimension_numbers=('NDHWC', 'DHWIO', 'NDHWC'), precision=lax.Precision.HIGHEST)
    return output[0]

def reference(latents, gain_in, weight_in, bias_in, gain_mid, weight_mid, bias_mid, up_weight, up_bias):
    widened = latents.astype(jnp.float32)
    inner = normed_silu(widened, gain_in).astype(jnp.bfloat16)
    mixed = causal_volume(inner, weight_in) + bias_in
    middle = normed_silu(mixed, gain_mid).astype(jnp.bfloat16)
    result = causal_volume(middle, weight_mid) + bias_mid
    summed = (widened + result).astype(jnp.bfloat16)
    enlarged = jnp.repeat(jnp.repeat(summed, 2, axis=1), 2, axis=2)
    padded = jnp.pad(enlarged.astype(jnp.float32), ((0, 0), (1, 1), (1, 1), (0, 0)))
    images = lax.conv_general_dilated(padded, up_weight.astype(jnp.float32), (1, 1), 'VALID', dimension_numbers=('NHWC', 'HWIO', 'NHWC'), precision=lax.Precision.HIGHEST)
    images = (images + up_bias).astype(jnp.bfloat16)
    return (images[0], images[1:])
```

```python
import functools

import jax
import jax.numpy as jnp
from jax import lax
from jax.experimental import pallas as pl
from jax.experimental.pallas import tpu as pltpu
from jax.sharding import PartitionSpec as P

epsilon = 1e-06
MESH = pl.DeviceIdType.MESH
AROUND = [(-1, 0), (1, 0), (0, -1), (0, 1), (-1, -1), (-1, 1), (1, -1), (1, 1)]


def rounded_up(count):
    return -(-count // 16) * 16


def normed_silu(values, norm_gain):
    factor = lax.rsqrt(jnp.mean(values * values, axis=-1, keepdims=True) + epsilon)
    return jax.nn.silu(values * factor * norm_gain)


def present(dh, dt, h, t, sizes):
    ok = (h + dh >= 0) & (h + dh < sizes[0])
    return ok & (t + dt >= 0) & (t + dt < sizes[1])


def spans_of(frames, rows, cols):
    lengths = [frames * cols] * 2 + [frames * rows] * 2 + [frames] * 4
    spans, start = [], 0
    for length in lengths:
        spans.append((start, length))
        start += rounded_up(length)
    return spans, start


def rim_pack(values):
    channels = values.shape[-1]
    pieces = []
    for dh, dt in AROUND:
        piece = values
        if dh:
            piece = piece[:, :1] if dh < 0 else piece[:, -1:]
        if dt:
            piece = piece[:, :, :1] if dt < 0 else piece[:, :, -1:]
        piece = piece.reshape(-1, channels)
        pieces.append(jnp.pad(piece, ((0, rounded_up(piece.shape[0]) - piece.shape[0]), (0, 0))))
    return jnp.concatenate(pieces, axis=0)


def rim_unpack(values, received):
    frames, rows, cols, channels = values.shape
    spans, _ = spans_of(frames, rows, cols)
    h, t = lax.axis_index("height"), lax.axis_index("tm")
    sizes = lax.axis_size("height"), lax.axis_size("tm")
    got = {}
    for (dh, dt), (start, length) in zip(AROUND, spans):
        piece = received[start : start + length].reshape(
            frames, 1 if dh else rows, 1 if dt else cols, channels
        )
        got[-dh, -dt] = jnp.where(present(-dh, -dt, h, t, sizes), piece, 0)
    lines = []
    for dh in (-1, 0, 1):
        middle = got[dh, 0] if dh else values
        lines.append(jnp.concatenate([got[dh, -1], middle, got[dh, 1]], axis=2))
    return jnp.concatenate(lines, axis=1)


def rim_kernel(spans, sizes, src, dst, send_sems, recv_sems):
    h, t = lax.axis_index("height"), lax.axis_index("tm")
    barrier = pltpu.get_barrier_semaphore()
    there = [present(dh, dt, h, t, sizes) for dh, dt in AROUND]
    for ok, (dh, dt) in zip(there, AROUND):

        @pl.when(ok)
        def _():
            pl.semaphore_signal(barrier, inc=1, device_id=(t + dt, h + dh), device_id_type=MESH)

    pl.semaphore_wait(barrier, sum(ok.astype(jnp.int32) for ok in there))

    def copy(k):
        dh, dt = AROUND[k]
        start, length = spans[k]
        part = pl.ds(start, rounded_up(length))
        return pltpu.make_async_remote_copy(
            src_ref=src.at[part],
            dst_ref=dst.at[part],
            send_sem=send_sems.at[k],
            recv_sem=recv_sems.at[k],
            device_id=(t + dt, h + dh),
            device_id_type=MESH,
        )

    for k in range(8):

        @pl.when(there[k])
        def _():
            copy(k).start()

    for k in range(8):

        @pl.when(there[k])
        def _():
            copy(k).wait_send()

    for k in range(8):
        dh, dt = AROUND[k]

        @pl.when(present(-dh, -dt, h, t, sizes))
        def _():
            copy(k).wait_recv()


def with_rim(values, collective_id):
    frames, rows, cols, channels = values.shape
    spans, total = spans_of(frames, rows, cols)
    sizes = lax.axis_size("height"), lax.axis_size("tm")
    received = pl.pallas_call(
        functools.partial(rim_kernel, spans, sizes),
        out_shape=jax.ShapeDtypeStruct((total, channels), values.dtype),
        in_specs=[pl.BlockSpec(memory_space=pl.ANY)],
        out_specs=pl.BlockSpec(memory_space=pl.ANY),
        scratch_shapes=[pltpu.SemaphoreType.DMA((8,)), pltpu.SemaphoreType.DMA((8,))],
        compiler_params=pltpu.CompilerParams(collective_id=collective_id, has_side_effects=True),
    )(rim_pack(values))
    return rim_unpack(values, received)


def spread_kernel(spans, cuts, sizes, first, later, first_out, later_out, fs, fr, ls, lr, own_sem):
    h, t = lax.axis_index("height"), lax.axis_index("tm")
    tops, groups = sizes
    barrier = pltpu.get_barrier_semaphore()
    row_there = {0: None, -1: h >= 1, 1: h + 1 < tops}
    partners = [(dh, j) for dh in (0, -1, 1) for j in range(groups) if (dh, j) != (0, 0)]

    def to(dh, j):
        return (lax.rem(t + j, groups), h + dh)

    def guarded(dh, action):
        if dh == 0:
            action()
        else:
            pl.when(row_there[dh])(action)

    for dh, j in partners:
        guarded(
            dh,
            lambda dh=dh, j=j: pl.semaphore_signal(
                barrier, inc=1, device_id=to(dh, j), device_id_type=MESH
            ),
        )
    lines = row_there[-1].astype(jnp.int32) + row_there[1].astype(jnp.int32)
    pl.semaphore_wait(barrier, groups - 1 + groups * lines)

    def later_copy(dh, j, slot):
        part = pl.ds(*cuts[dh])
        return pltpu.make_async_remote_copy(
            src_ref=later.at[lax.rem(t + j, groups), part],
            dst_ref=later_out.at[t, part],
            send_sem=ls.at[slot],
            recv_sem=lr.at[slot],
            device_id=to(dh, j),
            device_id_type=MESH,
        )

    def first_copy(k):
        dh, dt = AROUND[k]
        part = pl.ds(spans[k][0], rounded_up(spans[k][1]))
        return pltpu.make_async_remote_copy(
            src_ref=first.at[part],
            dst_ref=first_out.at[part],
            send_sem=fs.at[k],
            recv_sem=fr.at[k],
            device_id=(t + dt, h + dh),
            device_id_type=MESH,
        )

    for slot, (dh, j) in enumerate(partners):
        guarded(dh, lambda dh=dh, j=j, slot=slot: later_copy(dh, j, slot).start())
    for k in range(8):
        pl.when(present(*AROUND[k], h, t, sizes))(lambda k=k: first_copy(k).start())
    own = pltpu.make_async_copy(
        later.at[t, pl.ds(*cuts[0])], later_out.at[t, pl.ds(*cuts[0])], own_sem
    )
    own.start()
    own.wait()
    for slot, (dh, j) in enumerate(partners):
        guarded(dh, lambda dh=dh, j=j, slot=slot: later_copy(dh, j, slot).wait_send())
    for k in range(8):
        pl.when(present(*AROUND[k], h, t, sizes))(lambda k=k: first_copy(k).wait_send())
    for slot, (dh, j) in enumerate(partners):
        guarded(-dh, lambda dh=dh, j=j, slot=slot: later_copy(dh, j, slot).wait_recv())
    for k in range(8):
        dh, dt = AROUND[k]
        pl.when(present(-dh, -dt, h, t, sizes))(lambda k=k: first_copy(k).wait_recv())


def spread(summed):
    frames, rows, cols, channels = summed.shape
    groups = lax.axis_size("tm")
    sizes = lax.axis_size("height"), groups
    held = (frames - 1) // groups
    spans, total = spans_of(1, rows, cols)
    whole, line = held * rows * cols, held * cols
    cuts = {0: (0, whole), -1: (whole, line), 1: (whole + line, line)}
    blocks = summed[1:].reshape(groups, held, rows, cols, channels)
    later = jnp.concatenate(
        [
            blocks.reshape(groups, whole, channels),
            blocks[:, :, 0].reshape(groups, line, channels),
            blocks[:, :, -1].reshape(groups, line, channels),
        ],
        axis=1,
    )
    anywhere = pl.BlockSpec(memory_space=pl.ANY)
    count = 3 * groups - 1
    first_out, later_out = pl.pallas_call(
        functools.partial(spread_kernel, spans, cuts, sizes),
        out_shape=(
            jax.ShapeDtypeStruct((total, channels), summed.dtype),
            jax.ShapeDtypeStruct(later.shape, summed.dtype),
        ),
        in_specs=[anywhere] * 2,
        out_specs=(anywhere, anywhere),
        scratch_shapes=[
            pltpu.SemaphoreType.DMA((8,)),
            pltpu.SemaphoreType.DMA((8,)),
            pltpu.SemaphoreType.DMA((count,)),
            pltpu.SemaphoreType.DMA((count,)),
            pltpu.SemaphoreType.DMA,
        ],
        compiler_params=pltpu.CompilerParams(collective_id=2, has_side_effects=True),
    )(rim_pack(summed[:1]), later)
    first = rim_unpack(summed[:1], first_out)
    h = lax.axis_index("height")

    def lined(cut, count):
        part = later_out[:, cut[0] : cut[0] + cut[1]].reshape(groups, held, count, cols, channels)
        return part.transpose(1, 2, 0, 3, 4).reshape(held, count, groups * cols, channels)

    below = jnp.where(h + 1 < sizes[0], lined(cuts[-1], 1), 0)
    above = jnp.where(h >= 1, lined(cuts[1], 1), 0)
    block = jnp.concatenate([above, lined(cuts[0], rows), below], axis=1)
    return first, jnp.pad(block, ((0, 0), (0, 0), (1, 1), (0, 0)))


def row_taps(slab_rows, tap_weights):
    col_count = slab_rows.shape[-2] - 2
    widened = jnp.concatenate(
        [slab_rows[..., offset : offset + col_count, :] for offset in range(3)], axis=-1
    )
    merged = tap_weights.reshape(3 * tap_weights.shape[1], tap_weights.shape[2])
    return jnp.einsum("...c,cd->...d", widened, merged, preferred_element_type=jnp.float32)


def plane_conv(padded, tap_weights):
    row_count = padded.shape[-3] - 2
    summed = row_taps(padded[..., 0:row_count, :, :], tap_weights[0])
    for offset in range(1, 3):
        summed = summed + row_taps(
            padded[..., offset : offset + row_count, :, :], tap_weights[offset]
        )
    return summed


def causal_conv(padded, weight):
    frame_count = padded.shape[0] - 2
    summed = plane_conv(padded[0:frame_count], weight[0])
    for offset in range(1, 3):
        summed = summed + plane_conv(padded[offset : offset + frame_count], weight[offset])
    return summed


def brick_pad(values, collective_id):
    return jnp.pad(with_rim(values, collective_id), ((2, 0), (0, 0), (0, 0), (0, 0)))


def up_weights(up_weight):
    taps = up_weight.transpose(0, 3, 1, 2)
    taps = taps.reshape(3, taps.shape[1], -1)
    wide = taps.astype(jnp.float32)
    early = (wide[1] + wide[2]).astype(jnp.bfloat16)
    late = (wide[0] + wide[1]).astype(jnp.bfloat16)
    return (taps[0], early), (late, taps[2])


def enlarge_conv(padded, weights, up_bias):
    frames, padded_rows, padded_cols, channels = padded.shape
    rows, cols = padded_rows - 2, 2 * (padded_cols - 2)
    doubled = jnp.repeat(padded, 2, axis=2)[:, :, 1:-1]
    wide = jnp.concatenate([doubled[:, :, c : c + cols] for c in range(3)], axis=-1)
    halves = []
    for parity in range(2):
        half = up_bias
        for step in range(2):
            start = parity + step
            half = half + jnp.einsum(
                "frxc,oc->frxo",
                wide[:, start : start + rows],
                weights[parity][step],
                preferred_element_type=jnp.float32,
            )
        halves.append(half.astype(jnp.bfloat16))
    return jnp.stack(halves, axis=2).reshape(frames, 2 * rows, cols, -1)


def body(latents, gain_in, weight_in, bias_in, gain_mid, weight_mid, bias_mid, up_weight, up_bias):
    widened = latents.astype(jnp.float32)
    inner = normed_silu(widened, gain_in).astype(jnp.bfloat16)
    mixed = causal_conv(brick_pad(inner, 0), weight_in) + bias_in
    middle = normed_silu(mixed, gain_mid).astype(jnp.bfloat16)
    result = causal_conv(brick_pad(middle, 1), weight_mid) + bias_mid
    summed = (widened + result).astype(jnp.bfloat16)
    first, later = spread(summed)
    weights = up_weights(up_weight)
    return (enlarge_conv(first, weights, up_bias)[0], enlarge_conv(later, weights, up_bias))


def solution(mesh):
    return jax.shard_map(
        body,
        mesh=mesh,
        in_specs=(P(None, "height", "tm", None), P(), P(), P(), P(), P(), P(), P(), P()),
        out_specs=(P("height", "tm", None), P("tm", "height", None, None)),
        check_vma=False,
    )
```

```python
import functools

import jax
import jax.numpy as jnp
from jax import lax
from jax.experimental import pallas as pl
from jax.experimental.pallas import tpu as pltpu
from jax.sharding import PartitionSpec as P

epsilon = 1e-06
MESH = pl.DeviceIdType.MESH
AROUND = [(-1, 0), (1, 0), (0, -1), (0, 1), (-1, -1), (-1, 1), (1, -1), (1, 1)]


def rounded_up(count):
    return -(-count // 16) * 16


def normed_silu(values, norm_gain):
    factor = lax.rsqrt(jnp.mean(values * values, axis=-1, keepdims=True) + epsilon)
    scaled = values * factor * norm_gain
    return scaled / (1.0 + jnp.exp(-scaled))


def present(dh, dt, h, t, sizes):
    ok = (h + dh >= 0) & (h + dh < sizes[0])
    return ok & (t + dt >= 0) & (t + dt < sizes[1])


def spans_of(frames, rows, cols):
    lengths = [frames * cols] * 2 + [frames * rows] * 2 + [frames] * 4
    spans, start = [], 0
    for length in lengths:
        spans.append((start, length))
        start += rounded_up(length)
    return spans, start


def rim_pack(values):
    channels = values.shape[-1]
    pieces = []
    for dh, dt in AROUND:
        piece = values
        if dh:
            piece = piece[:, :1] if dh < 0 else piece[:, -1:]
        if dt:
            piece = piece[:, :, :1] if dt < 0 else piece[:, :, -1:]
        piece = piece.reshape(-1, channels)
        pieces.append(jnp.pad(piece, ((0, rounded_up(piece.shape[0]) - piece.shape[0]), (0, 0))))
    return jnp.concatenate(pieces, axis=0)


def rim_kernel(spans, sizes, src, dst, send_sems, recv_sems):
    h, t = lax.axis_index("height"), lax.axis_index("tm")
    barrier = pltpu.get_barrier_semaphore()
    there = [present(dh, dt, h, t, sizes) for dh, dt in AROUND]
    for ok, (dh, dt) in zip(there, AROUND):

        @pl.when(ok)
        def _():
            pl.semaphore_signal(barrier, inc=1, device_id=(t + dt, h + dh), device_id_type=MESH)

    pl.semaphore_wait(barrier, sum(ok.astype(jnp.int32) for ok in there))

    def copy(k):
        dh, dt = AROUND[k]
        start, length = spans[k]
        part = pl.ds(start, rounded_up(length))
        return pltpu.make_async_remote_copy(
            src_ref=src.at[part],
            dst_ref=dst.at[part],
            send_sem=send_sems.at[k],
            recv_sem=recv_sems.at[k],
            device_id=(t + dt, h + dh),
            device_id_type=MESH,
        )

    for k in range(8):

        @pl.when(there[k])
        def _():
            copy(k).start()

    for k in range(8):

        @pl.when(there[k])
        def _():
            copy(k).wait_send()

    for k in range(8):
        dh, dt = AROUND[k]

        @pl.when(present(-dh, -dt, h, t, sizes))
        def _():
            copy(k).wait_recv()


def exchanged(values, collective_id):
    frames, rows, cols, channels = values.shape
    spans, total = spans_of(frames, rows, cols)
    sizes = lax.axis_size("height"), lax.axis_size("tm")
    return pl.pallas_call(
        functools.partial(rim_kernel, spans, sizes),
        out_shape=jax.ShapeDtypeStruct((total, channels), values.dtype),
        in_specs=[pl.BlockSpec(memory_space=pl.ANY)],
        out_specs=pl.BlockSpec(memory_space=pl.ANY),
        scratch_shapes=[pltpu.SemaphoreType.DMA((8,)), pltpu.SemaphoreType.DMA((8,))],
        compiler_params=pltpu.CompilerParams(collective_id=collective_id, has_side_effects=True),
    )(rim_pack(values))


def spread_kernel(spans, line, sizes, first, later, first_out, later_out, edge_out, fs, fr, ls, lr, es, er, own_sem):
    h, t = lax.axis_index("height"), lax.axis_index("tm")
    tops, groups = sizes
    barrier = pltpu.get_barrier_semaphore()
    eight = [present(*way, h, t, sizes) for way in AROUND]
    ups = h >= 1, h + 1 < tops

    def to(j):
        return (lax.rem(t + j, groups), h)

    for j in range(1, groups):
        pl.semaphore_signal(barrier, inc=1, device_id=to(j), device_id_type=MESH)
    for k, (dh, dt) in enumerate(AROUND):
        if dh:

            @pl.when(eight[k])
            def _(dh=dh, dt=dt):
                pl.semaphore_signal(
                    barrier, inc=1, device_id=(t + dt, h + dh), device_id_type=MESH
                )

    pl.semaphore_wait(
        barrier,
        groups - 1 + sum(eight[k].astype(jnp.int32) for k in range(8) if AROUND[k][0]),
    )

    def later_copy(j):
        return pltpu.make_async_remote_copy(
            src_ref=later.at[lax.rem(t + j, groups)],
            dst_ref=later_out.at[t],
            send_sem=ls.at[j],
            recv_sem=lr.at[j],
            device_id=to(j),
            device_id_type=MESH,
        )

    def first_copy(k):
        dh, dt = AROUND[k]
        part = pl.ds(spans[k][0], rounded_up(spans[k][1]))
        return pltpu.make_async_remote_copy(
            src_ref=first.at[part],
            dst_ref=first_out.at[part],
            send_sem=fs.at[k],
            recv_sem=fr.at[k],
            device_id=(t + dt, h + dh),
            device_id_type=MESH,
        )

    def edge_copy(j, side):
        owner = lax.rem(t + groups - j, groups)
        start = 0 if side == 0 else later.shape[1] - line
        source = later.at[t] if j == 0 else later_out.at[owner]
        return pltpu.make_async_remote_copy(
            src_ref=source.at[pl.ds(start, line)],
            dst_ref=edge_out.at[side, owner],
            send_sem=es.at[side, j],
            recv_sem=er.at[side, j],
            device_id=(t, h + (-1 if side == 0 else 1)),
            device_id_type=MESH,
        )

    for j in (2, 1, 3) if groups == 4 else range(1, groups):
        later_copy(j).start()
    own = pltpu.make_async_copy(later.at[t], later_out.at[t], own_sem)
    own.start()
    for k in range(8):
        pl.when(eight[k])(lambda k=k: first_copy(k).start())
    for j in range(groups):
        if j:
            later_copy(j).wait_recv()
        for side in range(2):
            pl.when(ups[side])(lambda j=j, side=side: edge_copy(j, side).start())
    own.wait()
    for j in range(1, groups):
        later_copy(j).wait_send()
    for k in range(8):
        dh, dt = AROUND[k]
        pl.when(eight[k])(lambda k=k: first_copy(k).wait_send())
        pl.when(present(-dh, -dt, h, t, sizes))(lambda k=k: first_copy(k).wait_recv())
    for j in range(groups):
        for side in range(2):
            pl.when(ups[side])(lambda j=j, side=side: edge_copy(j, side).wait_send())
            pl.when(ups[1 - side])(lambda j=j, side=side: edge_copy(j, side).wait_recv())


def spread(summed):
    frames, rows, cols, channels = summed.shape
    groups = lax.axis_size("tm")
    sizes = lax.axis_size("height"), groups
    held = (frames - 1) // groups
    spans, total = spans_of(1, rows, cols)
    line = held * cols
    later = summed[1:].reshape(groups, held, rows, cols, channels).transpose(0, 2, 1, 3, 4)
    later = later.reshape(groups, rows * line, channels)
    anywhere = pl.BlockSpec(memory_space=pl.ANY)
    dma = pltpu.SemaphoreType.DMA
    return pl.pallas_call(
        functools.partial(spread_kernel, spans, line, sizes),
        out_shape=(
            jax.ShapeDtypeStruct((total, channels), summed.dtype),
            jax.ShapeDtypeStruct(later.shape, summed.dtype),
            jax.ShapeDtypeStruct((2, groups, line, channels), summed.dtype),
        ),
        in_specs=[anywhere] * 2,
        out_specs=(anywhere,) * 3,
        scratch_shapes=[dma((8,))] * 2 + [dma((groups,))] * 2 + [dma((2, groups))] * 2 + [dma],
        compiler_params=pltpu.CompilerParams(collective_id=2, has_side_effects=True),
    )(rim_pack(summed[:1]), later)


def rim_lines(values, rim, spans, sizes, frame):
    frames, rows, cols, channels = values.shape
    h, t = lax.axis_index("height"), lax.axis_index("tm")
    lines = []
    for r in range(rows + 2):
        dh = -1 if r == 0 else 1 if r == rows + 1 else 0

        def piece(dt, start_of, length):
            k = AROUND.index((-dh, -dt))
            base = spans[k][0] + start_of // 16 * 16
            size = rounded_up(length) if length > 1 else 16
            value = rim[base : base + size].astype(jnp.float32)
            value = value[start_of % 16 : start_of % 16 + length]
            return jnp.where(present(dh, dt, h, t, sizes), value, 0.0)

        if dh:
            line = piece(0, frame * cols, cols)
            sides = [piece(dt, frame, 1) for dt in (-1, 1)]
        else:
            line = values[frame, r - 1].astype(jnp.float32)
            sides = [piece(dt, frame * rows + r - 1, 1) for dt in (-1, 1)]
        lines.append((line, sides[0], sides[1]))
    return lines


def conv_kernel(spans, sizes, residual, x, rim, w, bias, other, out, buf, acc):
    frames, rows, cols, channels = x.shape
    step = pl.program_id(0)

    @pl.when(step == 0)
    def _():
        acc[...] = jnp.broadcast_to(bias[...], acc.shape)
        buf[:, 0:2] = jnp.zeros((3, 2, *buf.shape[2:]), buf.dtype)
        place = lax.broadcasted_iota(jnp.int32, (cols, channels), 0)
        for f in range(frames):
            for r, (line, left, right) in enumerate(rim_lines(x, rim, spans, sizes, f)):
                buf[0, f + 2, r] = jnp.where(place == 0, left, pltpu.roll(line, 1, 0)).astype(buf.dtype)
                buf[1, f + 2, r] = line.astype(buf.dtype)
                buf[2, f + 2, r] = jnp.where(
                    place == cols - 1, right, pltpu.roll(line, cols - 1, 0)
                ).astype(buf.dtype)

    a, b = step // 3, step % 3
    total = acc[...]
    for c in range(3):
        cells = buf[c, pl.ds(a, frames), pl.ds(b, rows)].reshape(frames * rows * cols, channels)
        total = total + jnp.dot(cells, w[0, 0, c], preferred_element_type=jnp.float32)
    acc[...] = total

    @pl.when(step == 8)
    def _():
        if residual:
            ended = other[...].reshape(acc.shape).astype(jnp.float32) + acc[...]
        else:
            ended = normed_silu(acc[...], other[...])
        out[...] = ended.astype(out.dtype).reshape(out.shape)


def conv(values, weight, bias, other, collective_id, residual):
    frames, rows, cols, channels = values.shape
    spans, _ = spans_of(frames, rows, cols)
    sizes = lax.axis_size("height"), lax.axis_size("tm")
    rim = exchanged(values, collective_id)
    bias = bias.reshape(1, channels)
    if not residual:
        other = other.reshape(1, channels)

    def whole(array):
        return pl.BlockSpec(array.shape, lambda i: (0,) * array.ndim)

    return pl.pallas_call(
        functools.partial(conv_kernel, spans, sizes, residual),
        out_shape=jax.ShapeDtypeStruct(values.shape, values.dtype),
        grid=(9,),
        in_specs=[
            whole(values),
            whole(rim),
            pl.BlockSpec((1, 1, *weight.shape[2:]), lambda i: (i // 3, i % 3, 0, 0, 0)),
            whole(bias),
            whole(other),
        ],
        out_specs=whole(values),
        scratch_shapes=[
            pltpu.VMEM((3, frames + 2, rows + 2, cols, channels), values.dtype),
            pltpu.VMEM((frames * rows * cols, channels), jnp.float32),
        ],
        compiler_params=pltpu.CompilerParams(vmem_limit_bytes=40 * 2**20),
    )(values, rim, weight, bias, other)


def doubling(cols, offset):
    at = lax.broadcasted_iota(jnp.int32, (2 * cols, cols), 0) + (offset - 1)
    source = 2 * lax.broadcasted_iota(jnp.int32, (2 * cols, cols), 1)
    return ((at == source) | (at == source + 1)).astype(jnp.bfloat16)


def up_kernel(spans, sizes, frame0, rim, later, edge, w, bias_row, bias_col, first_out, later_out):
    _, rows, cols, channels = frame0.shape
    groups = later.shape[0]
    held = later_out.shape[0]
    line = held * cols
    h = lax.axis_index("height")
    taps = {}
    for c in range(3):
        wide = [w[b, c].astype(jnp.float32) for b in range(3)]
        taps[0, 0, c], taps[1, 1, c] = w[0, c], w[2, c]
        taps[0, 1, c] = (wide[1] + wide[2]).astype(jnp.bfloat16)
        taps[1, 0, c] = (wide[0] + wide[1]).astype(jnp.bfloat16)
    last_dims = (((1,), (1,)), ((), ()))

    def doubled(matrix, values):
        return jnp.dot(matrix, values, preferred_element_type=jnp.float32)

    spreads = [doubling(groups * cols, c) for c in range(3)]
    for f in range(held):
        wide_rows = []
        for r in range(rows + 2):
            parts = []
            for s in range(groups):
                if r == 0:
                    part = jnp.where(h >= 1, edge[1, s, f * cols : (f + 1) * cols], 0)
                elif r == rows + 1:
                    part = jnp.where(h + 1 < sizes[0], edge[0, s, f * cols : (f + 1) * cols], 0)
                else:
                    start = (r - 1) * line + f * cols
                    part = later[s, start : start + cols]
                parts.append(part)
            whole = jnp.concatenate(parts, axis=0)
            wide_rows.append([doubled(m, whole).astype(jnp.bfloat16) for m in spreads])
        for r in range(rows):
            for parity in range(2):
                total = bias_col[...]
                for step in range(2):
                    for c in range(3):
                        total = total + lax.dot_general(
                            taps[parity, step, c],
                            wide_rows[r + parity + step][c],
                            last_dims,
                            preferred_element_type=jnp.float32,
                        )
                later_out[f, 2 * r + parity] = total.astype(later_out.dtype)

    spreads = [doubling(cols, c) for c in range(3)]
    place = lax.broadcasted_iota(jnp.int32, (2 * cols, channels), 0)
    wide_rows = []
    for cells, left, right in rim_lines(frame0, rim, spans, sizes, 0):
        wide = [doubled(m, cells.astype(jnp.bfloat16)) for m in spreads]
        wide[0] = jnp.where(place == 0, left, wide[0])
        wide[2] = jnp.where(place == 2 * cols - 1, right, wide[2])
        wide_rows.append([value.astype(jnp.bfloat16) for value in wide])
    for r in range(rows):
        for parity in range(2):
            total = bias_row[...]
            for step in range(2):
                for c in range(3):
                    total = total + lax.dot_general(
                        wide_rows[r + parity + step][c],
                        taps[parity, step, c],
                        last_dims,
                        preferred_element_type=jnp.float32,
                    )
            first_out[2 * r + parity] = total.astype(first_out.dtype)


def upsampled(summed, up_weight, up_bias):
    frames, rows, cols, channels = summed.shape
    groups = lax.axis_size("tm")
    sizes = lax.axis_size("height"), groups
    spans, _ = spans_of(1, rows, cols)
    rim, later, edge = spread(summed)
    held, outs = (frames - 1) // groups, up_weight.shape[-1]
    local = pl.BlockSpec(memory_space=pltpu.VMEM)
    first, images = pl.pallas_call(
        functools.partial(up_kernel, spans, sizes),
        out_shape=(
            jax.ShapeDtypeStruct((2 * rows, 2 * cols, outs), summed.dtype),
            jax.ShapeDtypeStruct((held, 2 * rows, outs, 2 * cols * groups), summed.dtype),
        ),
        in_specs=[local] * 7,
        out_specs=(local, local),
        compiler_params=pltpu.CompilerParams(vmem_limit_bytes=40 * 2**20),
    )(
        summed[:1],
        rim,
        later,
        edge,
        up_weight.transpose(0, 1, 3, 2),
        up_bias.reshape(1, outs),
        up_bias.reshape(outs, 1),
    )
    return first, images.transpose(0, 1, 3, 2)


def body(latents, gain_in, weight_in, bias_in, gain_mid, weight_mid, bias_mid, up_weight, up_bias):
    inner = normed_silu(latents.astype(jnp.float32), gain_in).astype(jnp.bfloat16)
    middle = conv(inner, weight_in, bias_in, gain_mid, 0, False)
    summed = conv(middle, weight_mid, bias_mid, latents, 1, True)
    return upsampled(summed, up_weight, up_bias)


def solution(mesh):
    return jax.shard_map(
        body,
        mesh=mesh,
        in_specs=(P(None, "height", "tm", None), P(), P(), P(), P(), P(), P(), P(), P()),
        out_specs=(P("height", "tm", None), P("tm", "height", None, None)),
        check_vma=False,
    )
```

```python
import functools

import jax
import jax.numpy as jnp
from jax import lax
from jax.experimental import pallas as pl
from jax.experimental.pallas import tpu as pltpu
from jax.sharding import PartitionSpec as P

epsilon = 1e-06
MESH = pl.DeviceIdType.MESH
AROUND = [(-1, 0), (1, 0), (0, -1), (0, 1), (-1, -1), (-1, 1), (1, -1), (1, 1)]


def rounded_up(count):
    return -(-count // 16) * 16


def normed_silu(values, norm_gain):
    factor = lax.rsqrt(jnp.mean(values * values, axis=-1, keepdims=True) + epsilon)
    scaled = values * factor * norm_gain
    return scaled / (1.0 + jnp.exp(-scaled))


def present(dh, dt, h, t, sizes):
    ok = (h + dh >= 0) & (h + dh < sizes[0])
    return ok & (t + dt >= 0) & (t + dt < sizes[1])


def spans_of(frames, rows, cols):
    lengths = [frames * cols] * 2 + [frames * rows] * 2 + [frames] * 4
    spans, start = [], 0
    for length in lengths:
        spans.append((start, length))
        start += rounded_up(length)
    return spans, start


def rim_pack(values):
    channels = values.shape[-1]
    pieces = []
    for dh, dt in AROUND:
        piece = values
        if dh:
            piece = piece[:, :1] if dh < 0 else piece[:, -1:]
        if dt:
            piece = piece[:, :, :1] if dt < 0 else piece[:, :, -1:]
        piece = piece.reshape(-1, channels)
        pieces.append(jnp.pad(piece, ((0, rounded_up(piece.shape[0]) - piece.shape[0]), (0, 0))))
    return jnp.concatenate(pieces, axis=0)


def rim_kernel(spans, sizes, src, dst, send_sems, recv_sems):
    h, t = lax.axis_index("height"), lax.axis_index("tm")
    barrier = pltpu.get_barrier_semaphore()
    there = [present(dh, dt, h, t, sizes) for dh, dt in AROUND]
    for ok, (dh, dt) in zip(there, AROUND):

        @pl.when(ok)
        def _():
            pl.semaphore_signal(barrier, inc=1, device_id=(t + dt, h + dh), device_id_type=MESH)

    pl.semaphore_wait(barrier, sum(ok.astype(jnp.int32) for ok in there))

    def copy(k):
        dh, dt = AROUND[k]
        start, length = spans[k]
        part = pl.ds(start, rounded_up(length))
        return pltpu.make_async_remote_copy(
            src_ref=src.at[part],
            dst_ref=dst.at[part],
            send_sem=send_sems.at[k],
            recv_sem=recv_sems.at[k],
            device_id=(t + dt, h + dh),
            device_id_type=MESH,
        )

    for k in range(8):

        @pl.when(there[k])
        def _():
            copy(k).start()

    for k in range(8):

        @pl.when(there[k])
        def _():
            copy(k).wait_send()

    for k in range(8):
        dh, dt = AROUND[k]

        @pl.when(present(-dh, -dt, h, t, sizes))
        def _():
            copy(k).wait_recv()


def spread_kernel(spans, line, sizes, first, later, first_out, later_out, edge_out, fs, fr, ls, lr, es, er, own_sem):
    h, t = lax.axis_index("height"), lax.axis_index("tm")
    tops, groups = sizes
    barrier = pltpu.get_barrier_semaphore()
    eight = [present(*way, h, t, sizes) for way in AROUND]
    ups = h >= 1, h + 1 < tops

    def to(j):
        return (lax.rem(t + j, groups), h)

    for j in range(1, groups):
        pl.semaphore_signal(barrier, inc=1, device_id=to(j), device_id_type=MESH)
    for k, (dh, dt) in enumerate(AROUND):
        if dh:

            @pl.when(eight[k])
            def _(dh=dh, dt=dt):
                pl.semaphore_signal(
                    barrier, inc=1, device_id=(t + dt, h + dh), device_id_type=MESH
                )

    pl.semaphore_wait(
        barrier,
        groups - 1 + sum(eight[k].astype(jnp.int32) for k in range(8) if AROUND[k][0]),
    )

    def later_copy(j):
        return pltpu.make_async_remote_copy(
            src_ref=later.at[lax.rem(t + j, groups)],
            dst_ref=later_out.at[t],
            send_sem=ls.at[j],
            recv_sem=lr.at[j],
            device_id=to(j),
            device_id_type=MESH,
        )

    def first_copy(k):
        dh, dt = AROUND[k]
        part = pl.ds(spans[k][0], rounded_up(spans[k][1]))
        return pltpu.make_async_remote_copy(
            src_ref=first.at[part],
            dst_ref=first_out.at[part],
            send_sem=fs.at[k],
            recv_sem=fr.at[k],
            device_id=(t + dt, h + dh),
            device_id_type=MESH,
        )

    def edge_copy(j, side):
        owner = lax.rem(t + groups - j, groups)
        start = 0 if side == 0 else later.shape[1] - line
        source = later.at[t] if j == 0 else later_out.at[owner]
        return pltpu.make_async_remote_copy(
            src_ref=source.at[pl.ds(start, line)],
            dst_ref=edge_out.at[side, owner],
            send_sem=es.at[side, j],
            recv_sem=er.at[side, j],
            device_id=(t, h + (-1 if side == 0 else 1)),
            device_id_type=MESH,
        )

    for j in (2, 1, 3) if groups == 4 else range(1, groups):
        later_copy(j).start()
    own = pltpu.make_async_copy(later.at[t], later_out.at[t], own_sem)
    own.start()
    for k in range(8):
        pl.when(eight[k])(lambda k=k: first_copy(k).start())
    for j in range(groups):
        if j:
            later_copy(j).wait_recv()
        for side in range(2):
            pl.when(ups[side])(lambda j=j, side=side: edge_copy(j, side).start())
    own.wait()
    for j in range(1, groups):
        later_copy(j).wait_send()
    for k in range(8):
        dh, dt = AROUND[k]
        pl.when(eight[k])(lambda k=k: first_copy(k).wait_send())
        pl.when(present(-dh, -dt, h, t, sizes))(lambda k=k: first_copy(k).wait_recv())
    for j in range(groups):
        for side in range(2):
            pl.when(ups[side])(lambda j=j, side=side: edge_copy(j, side).wait_send())
            pl.when(ups[1 - side])(lambda j=j, side=side: edge_copy(j, side).wait_recv())


def spread(summed):
    frames, rows, cols, channels = summed.shape
    groups = lax.axis_size("tm")
    sizes = lax.axis_size("height"), groups
    held = (frames - 1) // groups
    spans, total = spans_of(1, rows, cols)
    line = held * cols
    later = summed[1:].reshape(groups, held, rows, cols, channels).transpose(0, 2, 1, 3, 4)
    later = later.reshape(groups, rows * line, channels)
    anywhere = pl.BlockSpec(memory_space=pl.ANY)
    dma = pltpu.SemaphoreType.DMA
    return pl.pallas_call(
        functools.partial(spread_kernel, spans, line, sizes),
        out_shape=(
            jax.ShapeDtypeStruct((total, channels), summed.dtype),
            jax.ShapeDtypeStruct(later.shape, summed.dtype),
            jax.ShapeDtypeStruct((2, groups, line, channels), summed.dtype),
        ),
        in_specs=[anywhere] * 2,
        out_specs=(anywhere,) * 3,
        scratch_shapes=[dma((8,))] * 2 + [dma((groups,))] * 2 + [dma((2, groups))] * 2 + [dma],
        compiler_params=pltpu.CompilerParams(collective_id=2, has_side_effects=True),
    )(rim_pack(summed[:1]), later)


def rim_lines(values, rim, spans, sizes, frame):
    frames, rows, cols, channels = values.shape
    h, t = lax.axis_index("height"), lax.axis_index("tm")
    lines = []
    for r in range(rows + 2):
        dh = -1 if r == 0 else 1 if r == rows + 1 else 0

        def piece(dt, start_of, length):
            k = AROUND.index((-dh, -dt))
            base = spans[k][0] + start_of // 16 * 16
            size = rounded_up(length) if length > 1 else 16
            value = rim[base : base + size].astype(jnp.float32)
            value = value[start_of % 16 : start_of % 16 + length]
            return jnp.where(present(dh, dt, h, t, sizes), value, 0.0)

        if dh:
            line = piece(0, frame * cols, cols)
            sides = [piece(dt, frame, 1) for dt in (-1, 1)]
        else:
            line = values[frame, r - 1].astype(jnp.float32)
            sides = [piece(dt, frame * rows + r - 1, 1) for dt in (-1, 1)]
        lines.append((line, sides[0], sides[1]))
    return lines


def conv_kernel(
    spans, sizes, residual, x, packed, w, bias, other, out, buf, acc, rim, send_sems, recv_sems
):
    frames, rows, cols, channels = x.shape
    step = pl.program_id(0)

    @pl.when(step == 0)
    def _():
        rim_kernel(spans, sizes, packed, rim, send_sems, recv_sems)
        acc[...] = jnp.broadcast_to(bias[...], acc.shape)
        buf[:, 0:2] = jnp.zeros((3, 2, *buf.shape[2:]), buf.dtype)
        place = lax.broadcasted_iota(jnp.int32, (cols, channels), 0)
        for f in range(frames):
            for r, (line, left, right) in enumerate(rim_lines(x, rim, spans, sizes, f)):
                buf[0, f + 2, r] = jnp.where(place == 0, left, pltpu.roll(line, 1, 0)).astype(buf.dtype)
                buf[1, f + 2, r] = line.astype(buf.dtype)
                buf[2, f + 2, r] = jnp.where(
                    place == cols - 1, right, pltpu.roll(line, cols - 1, 0)
                ).astype(buf.dtype)

    a, b = step // 3, step % 3
    total = acc[...]
    for c in range(3):
        cells = buf[c, pl.ds(a, frames), pl.ds(b, rows)].reshape(frames * rows * cols, channels)
        total = total + jnp.dot(cells, w[0, 0, c], preferred_element_type=jnp.float32)
    acc[...] = total

    @pl.when(step == 8)
    def _():
        if residual:
            ended = other[...].reshape(acc.shape).astype(jnp.float32) + acc[...]
        else:
            ended = normed_silu(acc[...], other[...])
        out[...] = ended.astype(out.dtype).reshape(out.shape)


def conv(values, weight, bias, other, collective_id, residual):
    frames, rows, cols, channels = values.shape
    spans, total = spans_of(frames, rows, cols)
    sizes = lax.axis_size("height"), lax.axis_size("tm")
    packed = rim_pack(values)
    bias = bias.reshape(1, channels)
    if not residual:
        other = other.reshape(1, channels)

    def whole(array):
        return pl.BlockSpec(array.shape, lambda i: (0,) * array.ndim)

    return pl.pallas_call(
        functools.partial(conv_kernel, spans, sizes, residual),
        out_shape=jax.ShapeDtypeStruct(values.shape, values.dtype),
        grid=(9,),
        in_specs=[
            whole(values),
            whole(packed),
            pl.BlockSpec((1, 1, *weight.shape[2:]), lambda i: (i // 3, i % 3, 0, 0, 0)),
            whole(bias),
            whole(other),
        ],
        out_specs=whole(values),
        scratch_shapes=[
            pltpu.VMEM((3, frames + 2, rows + 2, cols, channels), values.dtype),
            pltpu.VMEM((frames * rows * cols, channels), jnp.float32),
            pltpu.VMEM((total, channels), values.dtype),
            pltpu.SemaphoreType.DMA((8,)),
            pltpu.SemaphoreType.DMA((8,)),
        ],
        compiler_params=pltpu.CompilerParams(
            collective_id=collective_id, has_side_effects=True, vmem_limit_bytes=58 * 2**20
        ),
    )(values, packed, weight, bias, other)


def doubling(cols, offset):
    at = lax.broadcasted_iota(jnp.int32, (2 * cols, cols), 0) + (offset - 1)
    source = 2 * lax.broadcasted_iota(jnp.int32, (2 * cols, cols), 1)
    return ((at == source) | (at == source + 1)).astype(jnp.bfloat16)


def up_kernel(spans, sizes, frame0, rim, later, edge, w, bias_row, bias_col, first_out, later_out):
    _, rows, cols, channels = frame0.shape
    groups = later.shape[0]
    held = later_out.shape[0]
    line = held * cols
    h = lax.axis_index("height")
    taps = {}
    for c in range(3):
        wide = [w[b, c].astype(jnp.float32) for b in range(3)]
        taps[0, 0, c], taps[1, 1, c] = w[0, c], w[2, c]
        taps[0, 1, c] = (wide[1] + wide[2]).astype(jnp.bfloat16)
        taps[1, 0, c] = (wide[0] + wide[1]).astype(jnp.bfloat16)
    last_dims = (((1,), (1,)), ((), ()))

    def doubled(matrix, values):
        return jnp.dot(matrix, values, preferred_element_type=jnp.float32)

    spreads = [doubling(groups * cols, c) for c in range(3)]
    for f in range(held):
        wide_rows = []
        for r in range(rows + 2):
            parts = []
            for s in range(groups):
                if r == 0:
                    part = jnp.where(h >= 1, edge[1, s, f * cols : (f + 1) * cols], 0)
                elif r == rows + 1:
                    part = jnp.where(h + 1 < sizes[0], edge[0, s, f * cols : (f + 1) * cols], 0)
                else:
                    start = (r - 1) * line + f * cols
                    part = later[s, start : start + cols]
                parts.append(part)
            whole = jnp.concatenate(parts, axis=0)
            wide_rows.append([doubled(m, whole).astype(jnp.bfloat16) for m in spreads])
        for r in range(rows):
            for parity in range(2):
                total = bias_col[...]
                for step in range(2):
                    for c in range(3):
                        total = total + lax.dot_general(
                            taps[parity, step, c],
                            wide_rows[r + parity + step][c],
                            last_dims,
                            preferred_element_type=jnp.float32,
                        )
                later_out[f, 2 * r + parity] = total.astype(later_out.dtype)

    spreads = [doubling(cols, c) for c in range(3)]
    place = lax.broadcasted_iota(jnp.int32, (2 * cols, channels), 0)
    wide_rows = []
    for cells, left, right in rim_lines(frame0, rim, spans, sizes, 0):
        wide = [doubled(m, cells.astype(jnp.bfloat16)) for m in spreads]
        wide[0] = jnp.where(place == 0, left, wide[0])
        wide[2] = jnp.where(place == 2 * cols - 1, right, wide[2])
        wide_rows.append([value.astype(jnp.bfloat16) for value in wide])
    for r in range(rows):
        for parity in range(2):
            total = bias_row[...]
            for step in range(2):
                for c in range(3):
                    total = total + lax.dot_general(
                        wide_rows[r + parity + step][c],
                        taps[parity, step, c],
                        last_dims,
                        preferred_element_type=jnp.float32,
                    )
            first_out[2 * r + parity] = total.astype(first_out.dtype)


def upsampled(summed, up_weight, up_bias):
    frames, rows, cols, channels = summed.shape
    groups = lax.axis_size("tm")
    sizes = lax.axis_size("height"), groups
    spans, _ = spans_of(1, rows, cols)
    rim, later, edge = spread(summed)
    held, outs = (frames - 1) // groups, up_weight.shape[-1]
    local = pl.BlockSpec(memory_space=pltpu.VMEM)
    first, images = pl.pallas_call(
        functools.partial(up_kernel, spans, sizes),
        out_shape=(
            jax.ShapeDtypeStruct((2 * rows, 2 * cols, outs), summed.dtype),
            jax.ShapeDtypeStruct((held, 2 * rows, outs, 2 * cols * groups), summed.dtype),
        ),
        in_specs=[local] * 7,
        out_specs=(local, local),
        compiler_params=pltpu.CompilerParams(vmem_limit_bytes=40 * 2**20),
    )(
        summed[:1],
        rim,
        later,
        edge,
        up_weight.transpose(0, 1, 3, 2),
        up_bias.reshape(1, outs),
        up_bias.reshape(outs, 1),
    )
    return first, images.transpose(0, 1, 3, 2)


def body(latents, gain_in, weight_in, bias_in, gain_mid, weight_mid, bias_mid, up_weight, up_bias):
    inner = normed_silu(latents.astype(jnp.float32), gain_in).astype(jnp.bfloat16)
    middle = conv(inner, weight_in, bias_in, gain_mid, 0, False)
    summed = conv(middle, weight_mid, bias_mid, latents, 1, True)
    return upsampled(summed, up_weight, up_bias)


def solution(mesh):
    return jax.shard_map(
        body,
        mesh=mesh,
        in_specs=(P(None, "height", "tm", None), P(), P(), P(), P(), P(), P(), P(), P()),
        out_specs=(P("height", "tm", None), P("tm", "height", None, None)),
        check_vma=False,
    )
```

```python
import functools

import jax
import jax.numpy as jnp
from jax import lax
from jax.experimental import pallas as pl
from jax.experimental.pallas import tpu as pltpu
from jax.sharding import PartitionSpec as P

epsilon = 1e-06
MESH = pl.DeviceIdType.MESH
AROUND = [(-1, 0), (1, 0), (0, -1), (0, 1), (-1, -1), (-1, 1), (1, -1), (1, 1)]


def rounded_up(count):
    return -(-count // 16) * 16


def normed_silu(values, norm_gain):
    factor = lax.rsqrt(jnp.mean(values * values, axis=-1, keepdims=True) + epsilon)
    scaled = values * factor * norm_gain
    return scaled / (1.0 + jnp.exp(-scaled))


def present(dh, dt, h, t, sizes):
    ok = (h + dh >= 0) & (h + dh < sizes[0])
    return ok & (t + dt >= 0) & (t + dt < sizes[1])


def spans_of(frames, rows, cols):
    lengths = [frames * cols] * 2 + [frames * rows] * 2 + [frames] * 4
    spans, start = [], 0
    for length in lengths:
        spans.append((start, length))
        start += rounded_up(length)
    return spans, start


def rim_pack(values):
    channels = values.shape[-1]
    pieces = []
    for dh, dt in AROUND:
        piece = values
        if dh:
            piece = piece[:, :1] if dh < 0 else piece[:, -1:]
        if dt:
            piece = piece[:, :, :1] if dt < 0 else piece[:, :, -1:]
        piece = piece.reshape(-1, channels)
        pieces.append(jnp.pad(piece, ((0, rounded_up(piece.shape[0]) - piece.shape[0]), (0, 0))))
    return jnp.concatenate(pieces, axis=0)


def rim_kernel(spans, sizes, src, dst, send_sems, recv_sems):
    h, t = lax.axis_index("height"), lax.axis_index("tm")
    barrier = pltpu.get_barrier_semaphore()
    there = [present(dh, dt, h, t, sizes) for dh, dt in AROUND]
    for ok, (dh, dt) in zip(there, AROUND):

        @pl.when(ok)
        def _():
            pl.semaphore_signal(barrier, inc=1, device_id=(t + dt, h + dh), device_id_type=MESH)

    pl.semaphore_wait(barrier, sum(ok.astype(jnp.int32) for ok in there))

    def copy(k):
        dh, dt = AROUND[k]
        start, length = spans[k]
        part = pl.ds(start, rounded_up(length))
        return pltpu.make_async_remote_copy(
            src_ref=src.at[part],
            dst_ref=dst.at[part],
            send_sem=send_sems.at[k],
            recv_sem=recv_sems.at[k],
            device_id=(t + dt, h + dh),
            device_id_type=MESH,
        )

    for k in range(8):

        @pl.when(there[k])
        def _():
            copy(k).start()

    for k in range(8):

        @pl.when(there[k])
        def _():
            copy(k).wait_send()

    for k in range(8):
        dh, dt = AROUND[k]

        @pl.when(present(-dh, -dt, h, t, sizes))
        def _():
            copy(k).wait_recv()


def spread_kernel(spans, line, sizes, first, later, first_out, later_out, edge_out, fs, fr, ls, lr, es, er, own_sem):
    h, t = lax.axis_index("height"), lax.axis_index("tm")
    tops, groups = sizes
    barrier = pltpu.get_barrier_semaphore()
    eight = [present(*way, h, t, sizes) for way in AROUND]
    ups = h >= 1, h + 1 < tops

    def to(j):
        return (lax.rem(t + j, groups), h)

    for j in range(1, groups):
        pl.semaphore_signal(barrier, inc=1, device_id=to(j), device_id_type=MESH)
    for k, (dh, dt) in enumerate(AROUND):
        if dh:

            @pl.when(eight[k])
            def _(dh=dh, dt=dt):
                pl.semaphore_signal(
                    barrier, inc=1, device_id=(t + dt, h + dh), device_id_type=MESH
                )

    pl.semaphore_wait(
        barrier,
        groups - 1 + sum(eight[k].astype(jnp.int32) for k in range(8) if AROUND[k][0]),
    )

    def later_copy(j):
        return pltpu.make_async_remote_copy(
            src_ref=later.at[lax.rem(t + j, groups)],
            dst_ref=later_out.at[t],
            send_sem=ls.at[j],
            recv_sem=lr.at[j],
            device_id=to(j),
            device_id_type=MESH,
        )

    def first_copy(k):
        dh, dt = AROUND[k]
        part = pl.ds(spans[k][0], rounded_up(spans[k][1]))
        return pltpu.make_async_remote_copy(
            src_ref=first.at[part],
            dst_ref=first_out.at[part],
            send_sem=fs.at[k],
            recv_sem=fr.at[k],
            device_id=(t + dt, h + dh),
            device_id_type=MESH,
        )

    def edge_copy(j, side):
        owner = lax.rem(t + groups - j, groups)
        start = 0 if side == 0 else later.shape[1] - line
        source = later.at[t] if j == 0 else later_out.at[owner]
        return pltpu.make_async_remote_copy(
            src_ref=source.at[pl.ds(start, line)],
            dst_ref=edge_out.at[side, owner],
            send_sem=es.at[side, j],
            recv_sem=er.at[side, j],
            device_id=(t, h + (-1 if side == 0 else 1)),
            device_id_type=MESH,
        )

    for j in (2, 1, 3) if groups == 4 else range(1, groups):
        later_copy(j).start()
    own = pltpu.make_async_copy(later.at[t], later_out.at[t], own_sem)
    own.start()
    for k in range(8):
        pl.when(eight[k])(lambda k=k: first_copy(k).start())
    for j in range(groups):
        if j:
            later_copy(j).wait_recv()
        for side in range(2):
            pl.when(ups[side])(lambda j=j, side=side: edge_copy(j, side).start())
    own.wait()
    for j in range(1, groups):
        later_copy(j).wait_send()
    for k in range(8):
        dh, dt = AROUND[k]
        pl.when(eight[k])(lambda k=k: first_copy(k).wait_send())
        pl.when(present(-dh, -dt, h, t, sizes))(lambda k=k: first_copy(k).wait_recv())
    for j in range(groups):
        for side in range(2):
            pl.when(ups[side])(lambda j=j, side=side: edge_copy(j, side).wait_send())
            pl.when(ups[1 - side])(lambda j=j, side=side: edge_copy(j, side).wait_recv())


def spread(summed):
    frames, rows, cols, channels = summed.shape
    groups = lax.axis_size("tm")
    sizes = lax.axis_size("height"), groups
    held = (frames - 1) // groups
    spans, total = spans_of(1, rows, cols)
    line = held * cols
    later = summed[1:].reshape(groups, held, rows, cols, channels).transpose(0, 2, 1, 3, 4)
    later = later.reshape(groups, rows * line, channels)
    anywhere = pl.BlockSpec(memory_space=pl.ANY)
    dma = pltpu.SemaphoreType.DMA
    return pl.pallas_call(
        functools.partial(spread_kernel, spans, line, sizes),
        out_shape=(
            jax.ShapeDtypeStruct((total, channels), summed.dtype),
            jax.ShapeDtypeStruct(later.shape, summed.dtype),
            jax.ShapeDtypeStruct((2, groups, line, channels), summed.dtype),
        ),
        in_specs=[anywhere] * 2,
        out_specs=(anywhere,) * 3,
        scratch_shapes=[dma((8,))] * 2 + [dma((groups,))] * 2 + [dma((2, groups))] * 2 + [dma],
        compiler_params=pltpu.CompilerParams(collective_id=2, has_side_effects=True),
    )(rim_pack(summed[:1]), later)


def rim_lines(values, rim, spans, sizes, frame):
    frames, rows, cols, channels = values.shape
    h, t = lax.axis_index("height"), lax.axis_index("tm")
    lines = []
    for r in range(rows + 2):
        dh = -1 if r == 0 else 1 if r == rows + 1 else 0

        def piece(dt, start_of, length):
            k = AROUND.index((-dh, -dt))
            base = spans[k][0] + start_of // 16 * 16
            size = rounded_up(length) if length > 1 else 16
            value = rim[base : base + size].astype(jnp.float32)
            value = value[start_of % 16 : start_of % 16 + length]
            return jnp.where(present(dh, dt, h, t, sizes), value, 0.0)

        if dh:
            line = piece(0, frame * cols, cols)
            sides = [piece(dt, frame, 1) for dt in (-1, 1)]
        else:
            line = values[frame, r - 1].astype(jnp.float32)
            sides = [piece(dt, frame * rows + r - 1, 1) for dt in (-1, 1)]
        lines.append((line, sides[0], sides[1]))
    return lines


def conv_kernel(
    spans, sizes, residual, x, packed, w, bias, other, out, buf, acc, rim, send_sems, recv_sems
):
    frames, rows, cols, channels = x.shape
    step = pl.program_id(0)

    @pl.when(step == 0)
    def _():
        rim_kernel(spans, sizes, packed, rim, send_sems, recv_sems)
        acc[...] = jnp.broadcast_to(bias[...], acc.shape)
        buf[:, 0:2] = jnp.zeros((3, 2, *buf.shape[2:]), buf.dtype)
        place = lax.broadcasted_iota(jnp.int32, (cols, channels), 0)
        for f in range(frames):
            for r, (line, left, right) in enumerate(rim_lines(x, rim, spans, sizes, f)):
                buf[0, f + 2, r] = jnp.where(place == 0, left, pltpu.roll(line, 1, 0)).astype(buf.dtype)
                buf[1, f + 2, r] = line.astype(buf.dtype)
                buf[2, f + 2, r] = jnp.where(
                    place == cols - 1, right, pltpu.roll(line, cols - 1, 0)
                ).astype(buf.dtype)

    a, b = step // 3, step % 3
    total = acc[...]
    for c in range(3):
        cells = buf[c, pl.ds(a, frames), pl.ds(b, rows)].reshape(frames * rows * cols, channels)
        total = total + jnp.dot(cells, w[0, 0, c], preferred_element_type=jnp.float32)
    acc[...] = total

    @pl.when(step == 8)
    def _():
        if residual:
            ended = other[...].reshape(acc.shape).astype(jnp.float32) + acc[...]
        else:
            ended = normed_silu(acc[...], other[...])
        out[...] = ended.astype(out.dtype).reshape(out.shape)


def conv(values, weight, bias, other, collective_id, residual):
    frames, rows, cols, channels = values.shape
    spans, total = spans_of(frames, rows, cols)
    sizes = lax.axis_size("height"), lax.axis_size("tm")
    packed = rim_pack(values)
    bias = bias.reshape(1, channels)
    if not residual:
        other = other.reshape(1, channels)

    def whole(array):
        return pl.BlockSpec(array.shape, lambda i: (0,) * array.ndim)

    return pl.pallas_call(
        functools.partial(conv_kernel, spans, sizes, residual),
        out_shape=jax.ShapeDtypeStruct(values.shape, values.dtype),
        grid=(9,),
        in_specs=[
            whole(values),
            whole(packed),
            pl.BlockSpec((1, 1, *weight.shape[2:]), lambda i: (i // 3, i % 3, 0, 0, 0)),
            whole(bias),
            whole(other),
        ],
        out_specs=whole(values),
        scratch_shapes=[
            pltpu.VMEM((3, frames + 2, rows + 2, cols, channels), values.dtype),
            pltpu.VMEM((frames * rows * cols, channels), jnp.float32),
            pltpu.VMEM((total, channels), values.dtype),
            pltpu.SemaphoreType.DMA((8,)),
            pltpu.SemaphoreType.DMA((8,)),
        ],
        compiler_params=pltpu.CompilerParams(
            collective_id=collective_id, has_side_effects=True, vmem_limit_bytes=53 * 2**20
        ),
    )(values, packed, weight, bias, other)


def doubling(cols, offset):
    at = lax.broadcasted_iota(jnp.int32, (2 * cols, cols), 0) + (offset - 1)
    source = 2 * lax.broadcasted_iota(jnp.int32, (2 * cols, cols), 1)
    return ((at == source) | (at == source + 1)).astype(jnp.bfloat16)


def up_kernel(spans, sizes, frame0, rim, later, edge, w, bias_row, bias_col, first_out, later_out):
    _, rows, cols, channels = frame0.shape
    groups = later.shape[0]
    held = later_out.shape[0]
    line = held * cols
    h = lax.axis_index("height")
    taps = {}
    for c in range(3):
        wide = [w[b, c].astype(jnp.float32) for b in range(3)]
        taps[0, 0, c], taps[1, 1, c] = w[0, c], w[2, c]
        taps[0, 1, c] = (wide[1] + wide[2]).astype(jnp.bfloat16)
        taps[1, 0, c] = (wide[0] + wide[1]).astype(jnp.bfloat16)
    last_dims = (((1,), (1,)), ((), ()))

    def doubled(matrix, values):
        return jnp.dot(matrix, values, preferred_element_type=jnp.float32)

    spreads = [doubling(groups * cols, c) for c in range(3)]
    for f in range(held):
        wide_rows = []
        for r in range(rows + 2):
            parts = []
            for s in range(groups):
                if r == 0:
                    part = jnp.where(h >= 1, edge[1, s, f * cols : (f + 1) * cols], 0)
                elif r == rows + 1:
                    part = jnp.where(h + 1 < sizes[0], edge[0, s, f * cols : (f + 1) * cols], 0)
                else:
                    start = (r - 1) * line + f * cols
                    part = later[s, start : start + cols]
                parts.append(part)
            whole = jnp.concatenate(parts, axis=0)
            wide_rows.append([doubled(m, whole).astype(jnp.bfloat16) for m in spreads])
        for r in range(rows):
            for parity in range(2):
                total = bias_col[...]
                for step in range(2):
                    for c in range(3):
                        total = total + lax.dot_general(
                            taps[parity, step, c],
                            wide_rows[r + parity + step][c],
                            last_dims,
                            preferred_element_type=jnp.float32,
                        )
                later_out[f, 2 * r + parity] = total.astype(later_out.dtype)

    spreads = [doubling(cols, c) for c in range(3)]
    place = lax.broadcasted_iota(jnp.int32, (2 * cols, channels), 0)
    wide_rows = []
    for cells, left, right in rim_lines(frame0, rim, spans, sizes, 0):
        wide = [doubled(m, cells.astype(jnp.bfloat16)) for m in spreads]
        wide[0] = jnp.where(place == 0, left, wide[0])
        wide[2] = jnp.where(place == 2 * cols - 1, right, wide[2])
        wide_rows.append([value.astype(jnp.bfloat16) for value in wide])
    for r in range(rows):
        for parity in range(2):
            total = bias_row[...]
            for step in range(2):
                for c in range(3):
                    total = total + lax.dot_general(
                        wide_rows[r + parity + step][c],
                        taps[parity, step, c],
                        last_dims,
                        preferred_element_type=jnp.float32,
                    )
            first_out[2 * r + parity] = total.astype(first_out.dtype)


def upsampled(summed, up_weight, up_bias):
    frames, rows, cols, channels = summed.shape
    groups = lax.axis_size("tm")
    sizes = lax.axis_size("height"), groups
    spans, _ = spans_of(1, rows, cols)
    rim, later, edge = spread(summed)
    held, outs = (frames - 1) // groups, up_weight.shape[-1]
    local = pl.BlockSpec(memory_space=pltpu.VMEM)
    first, images = pl.pallas_call(
        functools.partial(up_kernel, spans, sizes),
        out_shape=(
            jax.ShapeDtypeStruct((2 * rows, 2 * cols, outs), summed.dtype),
            jax.ShapeDtypeStruct((held, 2 * rows, outs, 2 * cols * groups), summed.dtype),
        ),
        in_specs=[local] * 7,
        out_specs=(local, local),
        compiler_params=pltpu.CompilerParams(vmem_limit_bytes=40 * 2**20),
    )(
        summed[:1],
        rim,
        later,
        edge,
        up_weight.transpose(0, 1, 3, 2),
        up_bias.reshape(1, outs),
        up_bias.reshape(outs, 1),
    )
    return first, images.transpose(0, 1, 3, 2)


def body(latents, gain_in, weight_in, bias_in, gain_mid, weight_mid, bias_mid, up_weight, up_bias):
    inner = normed_silu(latents.astype(jnp.float32), gain_in).astype(jnp.bfloat16)
    middle = conv(inner, weight_in, bias_in, gain_mid, 0, False)
    summed = conv(middle, weight_mid, bias_mid, latents, 1, True)
    return upsampled(summed, up_weight, up_bias)


def solution(mesh):
    return jax.shard_map(
        body,
        mesh=mesh,
        in_specs=(P(None, "height", "tm", None), P(), P(), P(), P(), P(), P(), P(), P()),
        out_specs=(P("height", "tm", None), P("tm", "height", None, None)),
        check_vma=False,
    )
```

```python
import functools

import jax
import jax.numpy as jnp
from jax import lax
from jax.experimental import pallas as pl
from jax.experimental.pallas import tpu as pltpu
from jax.sharding import PartitionSpec as P

epsilon = 1e-06
MESH = pl.DeviceIdType.MESH
AROUND = [(-1, 0), (1, 0), (0, -1), (0, 1), (-1, -1), (-1, 1), (1, -1), (1, 1)]


def rounded_up(count):
    return -(-count // 16) * 16


def normed_silu(values, norm_gain):
    factor = lax.rsqrt(jnp.mean(values * values, axis=-1, keepdims=True) + epsilon)
    scaled = values * factor * norm_gain
    return scaled / (1.0 + jnp.exp(-scaled))


def present(dh, dt, h, t, sizes):
    ok = (h + dh >= 0) & (h + dh < sizes[0])
    return ok & (t + dt >= 0) & (t + dt < sizes[1])


def spans_of(frames, rows, cols):
    lengths = [frames * cols] * 2 + [frames * rows] * 2 + [frames] * 4
    spans, start = [], 0
    for length in lengths:
        spans.append((start, length))
        start += rounded_up(length)
    return spans, start


def rim_pack(values):
    channels = values.shape[-1]
    pieces = []
    for dh, dt in AROUND:
        piece = values
        if dh:
            piece = piece[:, :1] if dh < 0 else piece[:, -1:]
        if dt:
            piece = piece[:, :, :1] if dt < 0 else piece[:, :, -1:]
        piece = piece.reshape(-1, channels)
        pieces.append(jnp.pad(piece, ((0, rounded_up(piece.shape[0]) - piece.shape[0]), (0, 0))))
    return jnp.concatenate(pieces, axis=0)


def rim_kernel(spans, sizes, src, dst, send_sems, recv_sems):
    h, t = lax.axis_index("height"), lax.axis_index("tm")
    barrier = pltpu.get_barrier_semaphore()
    there = [present(dh, dt, h, t, sizes) for dh, dt in AROUND]
    for ok, (dh, dt) in zip(there, AROUND):

        @pl.when(ok)
        def _():
            pl.semaphore_signal(barrier, inc=1, device_id=(t + dt, h + dh), device_id_type=MESH)

    pl.semaphore_wait(barrier, sum(ok.astype(jnp.int32) for ok in there))

    def copy(k):
        dh, dt = AROUND[k]
        start, length = spans[k]
        part = pl.ds(start, rounded_up(length))
        return pltpu.make_async_remote_copy(
            src_ref=src.at[part],
            dst_ref=dst.at[part],
            send_sem=send_sems.at[k],
            recv_sem=recv_sems.at[k],
            device_id=(t + dt, h + dh),
            device_id_type=MESH,
        )

    for k in range(8):

        @pl.when(there[k])
        def _():
            copy(k).start()

    for k in range(8):

        @pl.when(there[k])
        def _():
            copy(k).wait_send()

    for k in range(8):
        dh, dt = AROUND[k]

        @pl.when(present(-dh, -dt, h, t, sizes))
        def _():
            copy(k).wait_recv()


def spread_kernel(spans, line, sizes, first, later, first_out, later_out, edge_out, fs, fr, ls, lr, es, er, own_sem):
    h, t = lax.axis_index("height"), lax.axis_index("tm")
    tops, groups = sizes
    barrier = pltpu.get_barrier_semaphore()
    eight = [present(*way, h, t, sizes) for way in AROUND]
    ups = h >= 1, h + 1 < tops

    def to(j):
        return (lax.rem(t + j, groups), h)

    for j in range(1, groups):
        pl.semaphore_signal(barrier, inc=1, device_id=to(j), device_id_type=MESH)
    for k, (dh, dt) in enumerate(AROUND):
        if dh:

            @pl.when(eight[k])
            def _(dh=dh, dt=dt):
                pl.semaphore_signal(
                    barrier, inc=1, device_id=(t + dt, h + dh), device_id_type=MESH
                )

    pl.semaphore_wait(
        barrier,
        groups - 1 + sum(eight[k].astype(jnp.int32) for k in range(8) if AROUND[k][0]),
    )

    def later_copy(j):
        return pltpu.make_async_remote_copy(
            src_ref=later.at[lax.rem(t + j, groups)],
            dst_ref=later_out.at[t],
            send_sem=ls.at[j],
            recv_sem=lr.at[j],
            device_id=to(j),
            device_id_type=MESH,
        )

    def first_copy(k):
        dh, dt = AROUND[k]
        part = pl.ds(spans[k][0], rounded_up(spans[k][1]))
        return pltpu.make_async_remote_copy(
            src_ref=first.at[part],
            dst_ref=first_out.at[part],
            send_sem=fs.at[k],
            recv_sem=fr.at[k],
            device_id=(t + dt, h + dh),
            device_id_type=MESH,
        )

    def edge_copy(j, side):
        owner = lax.rem(t + groups - j, groups)
        start = 0 if side == 0 else later.shape[1] - line
        source = later.at[t] if j == 0 else later_out.at[owner]
        return pltpu.make_async_remote_copy(
            src_ref=source.at[pl.ds(start, line)],
            dst_ref=edge_out.at[side, owner],
            send_sem=es.at[side, j],
            recv_sem=er.at[side, j],
            device_id=(t, h + (-1 if side == 0 else 1)),
            device_id_type=MESH,
        )

    for j in (2, 1, 3) if groups == 4 else range(1, groups):
        later_copy(j).start()
    own = pltpu.make_async_copy(later.at[t], later_out.at[t], own_sem)
    own.start()
    for k in range(8):
        pl.when(eight[k])(lambda k=k: first_copy(k).start())
    for j in range(groups):
        if j:
            later_copy(j).wait_recv()
        for side in range(2):
            pl.when(ups[side])(lambda j=j, side=side: edge_copy(j, side).start())
    own.wait()
    for j in range(1, groups):
        later_copy(j).wait_send()
    for k in range(8):
        dh, dt = AROUND[k]
        pl.when(eight[k])(lambda k=k: first_copy(k).wait_send())
        pl.when(present(-dh, -dt, h, t, sizes))(lambda k=k: first_copy(k).wait_recv())
    for j in range(groups):
        for side in range(2):
            pl.when(ups[side])(lambda j=j, side=side: edge_copy(j, side).wait_send())
            pl.when(ups[1 - side])(lambda j=j, side=side: edge_copy(j, side).wait_recv())


def spread(summed):
    frames, rows, cols, channels = summed.shape
    groups = lax.axis_size("tm")
    sizes = lax.axis_size("height"), groups
    held = (frames - 1) // groups
    spans, total = spans_of(1, rows, cols)
    line = held * cols
    later = summed[1:].reshape(groups, held, rows, cols, channels).transpose(0, 2, 1, 3, 4)
    later = later.reshape(groups, rows * line, channels)
    anywhere = pl.BlockSpec(memory_space=pltpu.VMEM)
    dma = pltpu.SemaphoreType.DMA
    return pl.pallas_call(
        functools.partial(spread_kernel, spans, line, sizes),
        out_shape=(
            jax.ShapeDtypeStruct((total, channels), summed.dtype),
            jax.ShapeDtypeStruct(later.shape, summed.dtype),
            jax.ShapeDtypeStruct((2, groups, line, channels), summed.dtype),
        ),
        in_specs=[anywhere] * 2,
        out_specs=(anywhere,) * 3,
        scratch_shapes=[dma((8,))] * 2 + [dma((groups,))] * 2 + [dma((2, groups))] * 2 + [dma],
        compiler_params=pltpu.CompilerParams(collective_id=2, has_side_effects=True),
    )(rim_pack(summed[:1]), later)


def rim_lines(values, rim, spans, sizes, frame):
    frames, rows, cols, channels = values.shape
    h, t = lax.axis_index("height"), lax.axis_index("tm")
    lines = []
    for r in range(rows + 2):
        dh = -1 if r == 0 else 1 if r == rows + 1 else 0

        def piece(dt, start_of, length):
            k = AROUND.index((-dh, -dt))
            base = spans[k][0] + start_of // 16 * 16
            size = rounded_up(length) if length > 1 else 16
            value = rim[base : base + size].astype(jnp.float32)
            value = value[start_of % 16 : start_of % 16 + length]
            return jnp.where(present(dh, dt, h, t, sizes), value, 0.0)

        if dh:
            line = piece(0, frame * cols, cols)
            sides = [piece(dt, frame, 1) for dt in (-1, 1)]
        else:
            line = values[frame, r - 1].astype(jnp.float32)
            sides = [piece(dt, frame * rows + r - 1, 1) for dt in (-1, 1)]
        lines.append((line, sides[0], sides[1]))
    return lines


def conv_kernel(
    spans, sizes, residual, x, packed, w, bias, other, out, buf, acc, rim, send_sems, recv_sems
):
    frames, rows, cols, channels = x.shape
    step = pl.program_id(0)

    @pl.when(step == 0)
    def _():
        rim_kernel(spans, sizes, packed, rim, send_sems, recv_sems)
        acc[...] = jnp.broadcast_to(bias[...], acc.shape)
        buf[:, 0:2] = jnp.zeros((3, 2, *buf.shape[2:]), buf.dtype)
        place = lax.broadcasted_iota(jnp.int32, (cols, channels), 0)
        for f in range(frames):
            for r, (line, left, right) in enumerate(rim_lines(x, rim, spans, sizes, f)):
                buf[0, f + 2, r] = jnp.where(place == 0, left, pltpu.roll(line, 1, 0)).astype(buf.dtype)
                buf[1, f + 2, r] = line.astype(buf.dtype)
                buf[2, f + 2, r] = jnp.where(
                    place == cols - 1, right, pltpu.roll(line, cols - 1, 0)
                ).astype(buf.dtype)

    a, b = step // 3, step % 3
    total = acc[...]
    for c in range(3):
        cells = buf[c, pl.ds(a, frames), pl.ds(b, rows)].reshape(frames * rows * cols, channels)
        total = total + jnp.dot(cells, w[0, 0, c], preferred_element_type=jnp.float32)
    acc[...] = total

    @pl.when(step == 8)
    def _():
        if residual:
            ended = other[...].reshape(acc.shape).astype(jnp.float32) + acc[...]
        else:
            ended = normed_silu(acc[...], other[...])
        out[...] = ended.astype(out.dtype).reshape(out.shape)


def conv(values, weight, bias, other, collective_id, residual):
    frames, rows, cols, channels = values.shape
    spans, total = spans_of(frames, rows, cols)
    sizes = lax.axis_size("height"), lax.axis_size("tm")
    packed = rim_pack(values)
    bias = bias.reshape(1, channels)
    if not residual:
        other = other.reshape(1, channels)

    def whole(array):
        return pl.BlockSpec(array.shape, lambda i: (0,) * array.ndim)

    return pl.pallas_call(
        functools.partial(conv_kernel, spans, sizes, residual),
        out_shape=jax.ShapeDtypeStruct(values.shape, values.dtype),
        grid=(9,),
        in_specs=[
            whole(values),
            whole(packed),
            pl.BlockSpec((1, 1, *weight.shape[2:]), lambda i: (i // 3, i % 3, 0, 0, 0)),
            whole(bias),
            whole(other),
        ],
        out_specs=whole(values),
        scratch_shapes=[
            pltpu.VMEM((3, frames + 2, rows + 2, cols, channels), values.dtype),
            pltpu.VMEM((frames * rows * cols, channels), jnp.float32),
            pltpu.VMEM((total, channels), values.dtype),
            pltpu.SemaphoreType.DMA((8,)),
            pltpu.SemaphoreType.DMA((8,)),
        ],
        compiler_params=pltpu.CompilerParams(
            collective_id=collective_id, has_side_effects=True, vmem_limit_bytes=53 * 2**20
        ),
    )(values, packed, weight, bias, other)


def doubling(cols, offset):
    at = lax.broadcasted_iota(jnp.int32, (2 * cols, cols), 0) + (offset - 1)
    source = 2 * lax.broadcasted_iota(jnp.int32, (2 * cols, cols), 1)
    return ((at == source) | (at == source + 1)).astype(jnp.bfloat16)


def up_kernel(spans, sizes, frame0, rim, later, edge, w, bias_row, bias_col, first_out, later_out):
    _, rows, cols, channels = frame0.shape
    groups = later.shape[0]
    held = later_out.shape[0]
    line = held * cols
    h = lax.axis_index("height")
    taps = {}
    for c in range(3):
        wide = [w[b, c].astype(jnp.float32) for b in range(3)]
        taps[0, 0, c], taps[1, 1, c] = w[0, c], w[2, c]
        taps[0, 1, c] = (wide[1] + wide[2]).astype(jnp.bfloat16)
        taps[1, 0, c] = (wide[0] + wide[1]).astype(jnp.bfloat16)
    last_dims = (((1,), (1,)), ((), ()))

    def doubled(matrix, values):
        return jnp.dot(matrix, values, preferred_element_type=jnp.float32)

    spreads = [doubling(groups * cols, c) for c in range(3)]
    for f in range(held):
        wide_rows = []
        for r in range(rows + 2):
            parts = []
            for s in range(groups):
                if r == 0:
                    part = jnp.where(h >= 1, edge[1, s, f * cols : (f + 1) * cols], 0)
                elif r == rows + 1:
                    part = jnp.where(h + 1 < sizes[0], edge[0, s, f * cols : (f + 1) * cols], 0)
                else:
                    start = (r - 1) * line + f * cols
                    part = later[s, start : start + cols]
                parts.append(part)
            whole = jnp.concatenate(parts, axis=0)
            wide_rows.append([doubled(m, whole).astype(jnp.bfloat16) for m in spreads])
        for r in range(rows):
            for parity in range(2):
                total = bias_col[...]
                for step in range(2):
                    for c in range(3):
                        total = total + lax.dot_general(
                            taps[parity, step, c],
                            wide_rows[r + parity + step][c],
                            last_dims,
                            preferred_element_type=jnp.float32,
                        )
                later_out[f, 2 * r + parity] = total.astype(later_out.dtype)

    spreads = [doubling(cols, c) for c in range(3)]
    place = lax.broadcasted_iota(jnp.int32, (2 * cols, channels), 0)
    wide_rows = []
    for cells, left, right in rim_lines(frame0, rim, spans, sizes, 0):
        wide = [doubled(m, cells.astype(jnp.bfloat16)) for m in spreads]
        wide[0] = jnp.where(place == 0, left, wide[0])
        wide[2] = jnp.where(place == 2 * cols - 1, right, wide[2])
        wide_rows.append([value.astype(jnp.bfloat16) for value in wide])
    for r in range(rows):
        for parity in range(2):
            total = bias_row[...]
            for step in range(2):
                for c in range(3):
                    total = total + lax.dot_general(
                        wide_rows[r + parity + step][c],
                        taps[parity, step, c],
                        last_dims,
                        preferred_element_type=jnp.float32,
                    )
            first_out[2 * r + parity] = total.astype(first_out.dtype)


def upsampled(summed, up_weight, up_bias):
    frames, rows, cols, channels = summed.shape
    groups = lax.axis_size("tm")
    sizes = lax.axis_size("height"), groups
    spans, _ = spans_of(1, rows, cols)
    rim, later, edge = spread(summed)
    held, outs = (frames - 1) // groups, up_weight.shape[-1]
    local = pl.BlockSpec(memory_space=pltpu.VMEM)
    first, images = pl.pallas_call(
        functools.partial(up_kernel, spans, sizes),
        out_shape=(
            jax.ShapeDtypeStruct((2 * rows, 2 * cols, outs), summed.dtype),
            jax.ShapeDtypeStruct((held, 2 * rows, outs, 2 * cols * groups), summed.dtype),
        ),
        in_specs=[local] * 7,
        out_specs=(local, local),
        compiler_params=pltpu.CompilerParams(vmem_limit_bytes=40 * 2**20),
    )(
        summed[:1],
        rim,
        later,
        edge,
        up_weight.transpose(0, 1, 3, 2),
        up_bias.reshape(1, outs),
        up_bias.reshape(outs, 1),
    )
    return first, images.transpose(0, 1, 3, 2)


def body(latents, gain_in, weight_in, bias_in, gain_mid, weight_mid, bias_mid, up_weight, up_bias):
    inner = normed_silu(latents.astype(jnp.float32), gain_in).astype(jnp.bfloat16)
    middle = conv(inner, weight_in, bias_in, gain_mid, 0, False)
    summed = conv(middle, weight_mid, bias_mid, latents, 1, True)
    return upsampled(summed, up_weight, up_bias)


def solution(mesh):
    return jax.shard_map(
        body,
        mesh=mesh,
        in_specs=(P(None, "height", "tm", None), P(), P(), P(), P(), P(), P(), P(), P()),
        out_specs=(P("height", "tm", None), P("tm", "height", None, None)),
        check_vma=False,
    )
```
